256 devices in a mesh: mset: 16 (over x_hi, y, core), band: 16 (over x_lo, z).
Axes of the slice: x: 4 (x_hi: 2, x_lo: 2; x = x_hi * 2 + x_lo), y: 4, z: 8, core: 2. Of those that a mesh axis runs over, the one named last changes fastest.
Arguments:
- coeffs: bfloat16 [2, 704, 61440], P(None, 'band', 'mset'), may hold values from -6 to 6
- legendre: bfloat16 [640, 704, 2048], P('mset', None, 'band'), may hold values from -0.3125 to 0.3125
- wavenumber: int32 [640], P('mset'), may hold values from 0 to 639, as said below
- band_rows: int32 [16], P('band'), may hold values from 16 to 128, as said below
Outputs:
- fourier: bfloat16 [96, 1280, 2048], P('mset', None, 'band')
The draws below stay inside these ranges and needn't reach their ends.
Inputs may be any that keep to these rules, and one draw needn't show every extreme that they name: All entries differ; pair q stands for wavenumbers wavenumber[q] and 1279 - wavenumber[q]. Both ends of the range occur. `band_rows`: entries 2 j and 2 j + 1 are equal (a band and its mirror image); some band holds 128.
All inputs are finite; a program needn't handle non-finite values.
Results may differ from the reference program's by a relative error of at most 0.0051.
Values may be sent and summed in bfloat16 or wider, within the bound.
A program may use at most 128 MiB of HBM per device.

```python
import jax
import jax.numpy as jnp
from jax import lax

TRUNC = 1279
LAT_DEV = 128
ROWS = 704
PAIRS = 640
MTOTAL = 1280
FIELDS2 = 96
BANDS = 16
NLAT = 2048


def draw_wavenumber(key, part):
    half_count = (TRUNC + 1) // 2
    others = jax.random.permutation(key, half_count - 2).astype(jnp.int32) + 1
    chosen = jnp.concatenate([jnp.array([0, half_count - 1], dtype=jnp.int32), others[:PAIRS - 2]])
    order = jax.random.permutation(jax.random.fold_in(key, 7), PAIRS)
    return chosen[order]


def draw_band_rows(key, part):
    pair_bands = BANDS // 2
    band_counts = jax.random.randint(key, (pair_bands,), LAT_DEV // 8, LAT_DEV // 2 + 1, dtype=jnp.int32)
    fullest = jax.random.randint(jax.random.fold_in(key, 3), (), 0, pair_bands, dtype=jnp.int32)
    band_counts = jnp.where(jnp.arange(pair_bands, dtype=jnp.int32) == fullest, LAT_DEV, band_counts)
    return jnp.repeat(band_counts, 2).astype(jnp.int32)


def block_scale(rng, extent, shards, low, largest):
    gain, own = 1.0, jax.random.fold_in(rng, 6)
    for dim, parts in shards:
        steps = jnp.exp(jax.random.uniform(jax.random.fold_in(own, dim), (parts,), jnp.float32, low / len(shards), largest / len(shards)))
        gain = gain * jnp.repeat(steps, extent[dim] // parts).reshape([-1 if axis == dim else 1 for axis in range(len(extent))])
    return gain


def scatter_about(key, dims, width, reach, pieces=(), kind=jnp.bfloat16):
    values = width * jax.random.normal(key, dims, jnp.float32)
    if pieces:
        values = values * block_scale(key, dims, pieces, -0.22, 0.18)
    return jnp.clip(values, -reach, reach).astype(kind)


def setup_inputs(seed: int = 0) -> dict:
    key_of = jax.random.split(jax.random.key(seed), 5)
    return {
        "coeffs": scatter_about(key_of[0], (2, ROWS, PAIRS * FIELDS2), 1.0, 6.0, ((1, 16), (2, 16))),
        "legendre": scatter_about(key_of[1], (PAIRS, ROWS, NLAT), (ROWS // 2) ** -0.5, 0.3125, ((0, 16), (2, 16))),
        "wavenumber": draw_wavenumber(jax.random.fold_in(key_of[4], 71), 0),
        "band_rows": draw_band_rows(jax.random.fold_in(key_of[4], 71), 0),
    }


def reference(coeffs, legendre, wavenumber, band_rows):
    band_pairs = BANDS // 2
    lat_index = jnp.arange(NLAT, dtype=jnp.int32)
    valid_lat = (lat_index % LAT_DEV) < jnp.repeat(band_rows, LAT_DEV)
    row_index = jnp.arange(ROWS, dtype=jnp.int32)
    by_pair = jnp.transpose(coeffs.reshape(2, ROWS, PAIRS, FIELDS2), (2, 0, 1, 3))

    def one_pair(inputs):
        coeff_pair, legendre_pair, smaller = inputs
        shaped = legendre_pair.reshape(ROWS, band_pairs, 2, LAT_DEV)
        parity_sums = []
        for parity in range(2):
            first_count = jnp.maximum((TRUNC - smaller - parity) // 2 + 1, 0)
            second_count = jnp.maximum((smaller - parity) // 2 + 1, 0)
            in_first = row_index < first_count
            in_second = jnp.logical_and(jnp.logical_not(in_first), row_index < first_count + second_count)
            rows_here = coeff_pair[parity]
            nothing = jnp.zeros((), rows_here.dtype)
            stacked = jnp.concatenate([jnp.where(in_first[:, None], rows_here, nothing), jnp.where(in_second[:, None], rows_here, nothing)], axis=1)
            columns = shaped[:, :, parity, :].reshape(ROWS, band_pairs * LAT_DEV)
            part_sum = jnp.dot(stacked.T, columns, preferred_element_type=jnp.float32).astype(jnp.bfloat16)
            parity_sums.append(lax.optimization_barrier(part_sum).astype(jnp.float32))
        even_part = parity_sums[0].reshape(2 * FIELDS2, band_pairs, LAT_DEV)
        odd_part = parity_sums[1].reshape(2 * FIELDS2, band_pairs, LAT_DEV)
        hemispheres = jnp.stack([even_part + odd_part, even_part - odd_part], axis=2).reshape(2 * FIELDS2, NLAT)
        hemispheres = jnp.where(valid_lat[None, :], hemispheres, jnp.zeros((), hemispheres.dtype)).astype(jnp.bfloat16)
        return hemispheres.reshape(2, FIELDS2, NLAT)

    result = lax.map(one_pair, (by_pair, legendre, wavenumber))
    return jnp.transpose(result.reshape(MTOTAL, FIELDS2, NLAT), (1, 0, 2))
```

```python
import jax
import jax.numpy as jnp
from jax import lax
from jax.experimental import pallas as pl
from jax.experimental.pallas import tpu as pltpu
from jax.sharding import PartitionSpec as P

TRUNC = 1279
MESH = pl.DeviceIdType.MESH
CHUNKS = 5
GROUPS = 2
QUAD = 4
FIELDS = 96
SLOT_ROWS = 48
SLOTS = 16 * GROUPS * QUAD // 8
OFFSETS = (0, -1, 1, -2, 2, -3, 3, 4)


def first_row(band):
    return 44 * band - 4 * (band % 2)


def kernel(
    cin, first_ref, total_ref, rows_ref, legendre, out,
    held, leg, turned, stage, esend, erecv, asend,
    leg_sem, own_sem, z_send, z_recv, x_send, x_recv, e_send, e_recv, a_send, a_recv, self_sem,
):
    s = lax.axis_index("mset")
    b = lax.axis_index("band")
    xl, z = b // 8, b % 8
    parity = z % 2

    def at_z(offset):
        return lax.rem(z + (8 + offset), 8)

    def on_line(offset):
        return (s, xl * 8 + at_z(offset))

    def own_slot(offset):
        return xl * 8 + at_z(offset)

    across = (s, (1 - xl) * 8 + z)
    mirror = (s, xl * 8 + z + 1 - 2 * parity)

    barrier = pltpu.get_barrier_semaphore()
    for device in (on_line(-2), on_line(-1), on_line(1), on_line(2), across):
        pl.semaphore_signal(barrier, inc=1, device_id=device, device_id_type=MESH)

    def greet(d, carry):
        pl.semaphore_signal(barrier, inc=1, device_id=(lax.rem(s + d, 16), b), device_id_type=MESH)
        return carry

    lax.fori_loop(1, 16, greet, 0)

    def leg_copy(k):
        pairs = pl.ds(k * GROUPS * QUAD, GROUPS * QUAD)
        return pltpu.make_async_copy(legendre.at[pairs], leg.at[pairs], leg_sem.at[k])

    for k in range(CHUNKS):
        leg_copy(k).start()
    own_copy = pltpu.make_async_copy(cin.at[parity], held.at[own_slot(0)], own_sem)
    own_copy.start()
    pl.semaphore_wait(barrier, 20)

    def whole(k):
        return pl.ds(k * GROUPS, GROUPS)

    def half(k, i):
        return pl.ds(k * GROUPS + i * (GROUPS // 2), GROUPS // 2)

    def z_copy(kind, k):
        if kind == 0:
            src, block, target, cols = cin.at[parity, whole(k)], 0, 2, whole(k)
        elif kind == 1:
            src, block, target, cols = cin.at[parity, whole(k)], 0, -2, whole(k)
        elif kind == 2:
            src, block, target, cols = cin.at[1 - parity, whole(k)], 0, 1, whole(k)
        elif kind == 3:
            src, block, target, cols = cin.at[1 - parity, whole(k)], 0, -1, whole(k)
        else:
            block, target, cols = {
                4: (-1, 2, whole(k)),
                5: (1, -2, whole(k)),
                6: (-2, 2, half(k, 0)),
                7: (2, -2, half(k, 1)),
            }[kind]
            src = held.at[own_slot(block), cols]
        return pltpu.make_async_remote_copy(
            src_ref=src,
            dst_ref=held.at[own_slot(block), cols],
            send_sem=z_send.at[kind, k],
            recv_sem=z_recv.at[kind, k],
            device_id=on_line(target),
            device_id_type=MESH,
        )

    def z_arrival(kind, k):
        block, cols = {
            0: (-2, whole(k)),
            1: (2, whole(k)),
            2: (-1, whole(k)),
            3: (1, whole(k)),
            4: (-3, whole(k)),
            5: (3, whole(k)),
            6: (4, half(k, 0)),
            7: (4, half(k, 1)),
        }[kind]
        here = held.at[own_slot(block), cols]
        return pltpu.make_async_copy(here, here, z_recv.at[kind, k])

    def x_copy(j, k):
        slot = own_slot(OFFSETS[j])
        src = cin.at[parity, whole(k)] if j == 0 else held.at[slot, whole(k)]
        return pltpu.make_async_remote_copy(
            src_ref=src,
            dst_ref=held.at[slot, whole(k)],
            send_sem=x_send.at[j, k],
            recv_sem=x_recv.at[j, k],
            device_id=across,
            device_id_type=MESH,
        )

    def x_arrival(j, k):
        here = held.at[(1 - xl) * 8 + at_z(OFFSETS[j]), whole(k)]
        return pltpu.make_async_copy(here, here, x_recv.at[j, k])

    def e_copy(k):
        return pltpu.make_async_remote_copy(
            src_ref=esend.at[k],
            dst_ref=erecv.at[k],
            send_sem=e_send.at[k],
            recv_sem=e_recv.at[k],
            device_id=mirror,
            device_id_type=MESH,
        )

    def out_rows(k):
        return pl.ds(pl.multiple_of(s * (CHUNKS * SLOTS) + k * SLOTS, SLOTS), SLOTS)

    def self_copy(k):
        return pltpu.make_async_copy(asend.at[k, pl.ds(s * 6, 6)], out.at[:, out_rows(k), :], self_sem.at[k])

    def direct(k):
        for kind in range(4):
            z_copy(kind, k).start()
        x_copy(0, k).start()

    def forward(k):
        for kind in (2, 3, 0, 1):
            z_arrival(kind, k).wait()
            z_copy({2: 4, 3: 5, 0: 6, 1: 7}[kind], k).start()
            x_copy({2: 1, 3: 2, 0: 3, 1: 4}[kind], k).start()

    def last(k):
        z_arrival(4, k).wait()
        x_copy(5, k).start()
        z_arrival(5, k).wait()
        x_copy(6, k).start()
        z_arrival(6, k).wait()
        z_arrival(7, k).wait()
        x_copy(7, k).start()

    def transform(k):
        for j in range(8):
            x_arrival(j, k).wait()
        leg_copy(k).wait()

        def group(i, carry):
            g = k * GROUPS + i
            turned[...] = held[:, g].reshape(16 * SLOT_ROWS, QUAD * FIELDS).T
            for n in range(QUAD):
                q = g * QUAD + n
                first, total = first_ref[q], total_ref[q]
                low, high = [], []
                for band in range(16):
                    row = lax.broadcasted_iota(jnp.int32, (SLOT_ROWS, 128), 0) + first_row(band)
                    piece = leg[q, pl.ds(first_row(band), SLOT_ROWS), :]
                    zero = jnp.zeros_like(piece)
                    low.append(jnp.where(row < first, piece, zero))
                    high.append(jnp.where((row >= first) & (row < total), piece, zero))
                basis = jnp.concatenate([jnp.concatenate(low, 0), jnp.concatenate(high, 0)], 1)
                sums = jnp.dot(
                    turned[pl.ds(n * FIELDS, FIELDS), :], basis, preferred_element_type=jnp.float32
                )
                slot = i * (2 * QUAD) + 2 * n
                stage[pl.ds(slot, FIELDS, stride=SLOTS), :] = sums[:, :128]
                stage[pl.ds(slot + 1, FIELDS, stride=SLOTS), :] = sums[:, 128:]
            return carry

        lax.fori_loop(0, GROUPS, group, 0)
        esend[k] = stage[...].astype(jnp.bfloat16).reshape(FIELDS, SLOTS, 128)
        e_copy(k).start()

    def combine(k):
        e_copy(k).wait_recv()
        own = esend[k].astype(jnp.float32)
        partner = erecv[k].astype(jnp.float32)
        sign = jnp.where(parity == 0, 1.0, -1.0).astype(jnp.float32)
        grid = partner + sign * own
        lane = lax.broadcasted_iota(jnp.int32, grid.shape, 2)
        asend[k] = jnp.where(lane < rows_ref[0], grid, 0.0).astype(jnp.bfloat16)
        self_copy(k).start()

        def send(d, carry):
            t = lax.rem(s + d, 16)
            pltpu.make_async_remote_copy(
                src_ref=asend.at[k, pl.ds(t * 6, 6)],
                dst_ref=out.at[:, out_rows(k), :],
                send_sem=a_send,
                recv_sem=a_recv,
                device_id=(t, b),
                device_id_type=MESH,
            ).start()
            return carry

        lax.fori_loop(1, 16, send, 0)

    own_copy.wait()

    def step(i, carry):
        for delay, stage_of in enumerate((direct, forward, last, transform, combine)):
            k = i - delay

            @pl.when((k >= 0) & (k < CHUNKS))
            def _(k=k, stage_of=stage_of):
                stage_of(k)

        return carry

    lax.fori_loop(0, CHUNKS + 4, step, 0)

    def finish(k, carry):
        for kind in range(8):
            z_copy(kind, k).wait_send()
        for j in range(8):
            x_copy(j, k).wait_send()
        e_copy(k).wait_send()
        self_copy(k).wait()
        return carry

    lax.fori_loop(0, CHUNKS, finish, 0)
    sent = asend.at[:, pl.ds(0, 90)]
    pltpu.make_async_copy(sent, sent, a_send).wait()
    got = out.at[:, pl.ds(0, 15 * CHUNKS * SLOTS), :]
    pltpu.make_async_copy(got, got, a_recv).wait()


def shards(coeffs, legendre, wavenumber, band_rows):
    band = lax.axis_index("band")
    parity = band % 2
    first = jnp.maximum((TRUNC - wavenumber - parity) // 2 + 1, 0)
    total = first + jnp.maximum((wavenumber - parity) // 2 + 1, 0)
    blocks = CHUNKS * GROUPS
    split = jnp.swapaxes(coeffs.reshape(2, 44, blocks, QUAD * FIELDS), 1, 2)
    pads = [jnp.pad(split, ((0, 0), (0, 0), ends, (0, 0))) for ends in ((0, 4), (4, 0))]
    cin = jnp.where(parity == 0, pads[0], pads[1])
    vmem = pl.BlockSpec(memory_space=pltpu.VMEM)
    smem = pl.BlockSpec(memory_space=pltpu.SMEM)
    anywhere = pl.BlockSpec(memory_space=pl.ANY)
    dma = pltpu.SemaphoreType.DMA
    sums = (CHUNKS, FIELDS, SLOTS, 128)
    return pl.pallas_call(
        kernel,
        out_shape=jax.ShapeDtypeStruct((6, 16 * CHUNKS * SLOTS, 128), jnp.bfloat16),
        in_specs=[vmem, smem, smem, smem, anywhere],
        out_specs=anywhere,
        scratch_shapes=[
            pltpu.VMEM((16, blocks, SLOT_ROWS, QUAD * FIELDS), jnp.bfloat16),
            pltpu.VMEM(legendre.shape, jnp.bfloat16),
            pltpu.VMEM((QUAD * FIELDS, 16 * SLOT_ROWS), jnp.bfloat16),
            pltpu.VMEM((FIELDS * SLOTS, 128), jnp.float32),
            pltpu.VMEM(sums, jnp.bfloat16),
            pltpu.VMEM(sums, jnp.bfloat16),
            pltpu.VMEM(sums, jnp.bfloat16),
            dma((CHUNKS,)),
            dma,
            dma((8, CHUNKS)),
            dma((8, CHUNKS)),
            dma((8, CHUNKS)),
            dma((8, CHUNKS)),
            dma((CHUNKS,)),
            dma((CHUNKS,)),
            dma,
            dma,
            dma((CHUNKS,)),
        ],
        compiler_params=pltpu.CompilerParams(
            collective_id=0, has_side_effects=True, vmem_limit_bytes=48 * 1024 * 1024
        ),
        cost_estimate=pl.CostEstimate(
            flops=2 * 40 * 768 * 96 * 256, bytes_accessed=20_000_000, transcendentals=0
        ),
    )(cin, first, total, band_rows, legendre)


def solution(mesh):
    in_specs = (P(None, "band", "mset"), P("mset", None, "band"), P("mset"), P("band"))
    out_specs = P("mset", None, "band")
    return jax.shard_map(shards, mesh=mesh, in_specs=in_specs, out_specs=out_specs, check_vma=False)
```

```python
import jax
import jax.numpy as jnp
from jax import lax
from jax.experimental import pallas as pl
from jax.experimental.pallas import tpu as pltpu
from jax.sharding import PartitionSpec as P

TRUNC = 1279
MESH = pl.DeviceIdType.MESH
CHUNKS = 5
GROUPS = 2
QUAD = 4
FIELDS = 96
ROWS = 704
MAIN = 40
BLOCK = 2 * MAIN + 8
SLOTS = 2 * GROUPS * QUAD
PIECES = 4
OFFSETS = (0, -1, 1, -2, 2, -3, 3, 4)


def kernel(
    cin, first_ref, total_ref, rows_ref, legendre, out,
    held, leg, natural, turned, stage, esend, erecv, asend,
    leg_sem, own_sem, z_send, z_recv, x_send, x_recv, e_send, e_recv, a_send, a_recv, self_sem,
):
    s = lax.axis_index("mset")
    b = lax.axis_index("band")
    xl, z = b // 8, b % 8
    parity = z % 2

    def at_z(offset):
        return lax.rem(z + (8 + offset), 8)

    def on_line(offset):
        return (s, xl * 8 + at_z(offset))

    def own_slot(offset):
        return xl * 8 + at_z(offset)

    across = (s, (1 - xl) * 8 + z)
    mirror = (s, xl * 8 + z + 1 - 2 * parity)

    barrier = pltpu.get_barrier_semaphore()
    for device in (on_line(-2), on_line(-1), on_line(1), on_line(2), across):
        pl.semaphore_signal(barrier, inc=1, device_id=device, device_id_type=MESH)

    def greet(d, carry):
        pl.semaphore_signal(barrier, inc=1, device_id=(lax.rem(s + d, 16), b), device_id_type=MESH)
        return carry

    lax.fori_loop(1, 16, greet, 0)

    def leg_copy(k):
        pairs = pl.ds(k * GROUPS * QUAD, GROUPS * QUAD)
        return pltpu.make_async_copy(legendre.at[pairs], leg.at[pairs], leg_sem.at[k])

    for k in range(CHUNKS):
        leg_copy(k).start()
    own_copy = pltpu.make_async_copy(cin.at[parity], held.at[own_slot(0)], own_sem)
    own_copy.start()
    pl.semaphore_wait(barrier, 20)

    def z_copy(kind, k):
        if kind == 4:
            way = 1 - 2 * lax.rem(k + s, 2)
            block, target = -2 * way, 2 * way
        else:
            block, target = {0: (0, 2), 1: (0, -2), 2: (0, 1), 3: (0, -1), 5: (-1, 2), 6: (1, -2)}[kind]
        if kind in (0, 1):
            src = cin.at[parity, k]
        elif kind in (2, 3):
            src = cin.at[1 - parity, k]
        else:
            src = held.at[own_slot(block), k]
        return pltpu.make_async_remote_copy(
            src_ref=src,
            dst_ref=held.at[own_slot(block), k],
            send_sem=z_send.at[kind, k],
            recv_sem=z_recv.at[kind, k],
            device_id=on_line(target),
            device_id_type=MESH,
        )

    def z_arrival(kind, k):
        block = {0: -2, 1: 2, 2: -1, 3: 1, 4: 4, 5: -3, 6: 3}[kind]
        here = held.at[own_slot(block), k]
        return pltpu.make_async_copy(here, here, z_recv.at[kind, k])

    def x_copy(j, k):
        slot = own_slot(OFFSETS[j])
        return pltpu.make_async_remote_copy(
            src_ref=cin.at[parity, k] if j == 0 else held.at[slot, k],
            dst_ref=held.at[slot, k],
            send_sem=x_send.at[j, k],
            recv_sem=x_recv.at[j, k],
            device_id=across,
            device_id_type=MESH,
        )

    def x_arrival(j, k):
        here = held.at[(1 - xl) * 8 + at_z(OFFSETS[j]), k]
        return pltpu.make_async_copy(here, here, x_recv.at[j, k])

    def e_copy(k, piece):
        return pltpu.make_async_remote_copy(
            src_ref=esend.at[k, piece],
            dst_ref=erecv.at[k, piece],
            send_sem=e_send.at[k, piece],
            recv_sem=e_recv.at[k, piece],
            device_id=mirror,
            device_id_type=MESH,
        )

    def out_rows(k):
        return pl.ds(pl.multiple_of(s * (CHUNKS * SLOTS) + k * SLOTS, SLOTS), SLOTS)

    def self_copy(k):
        return pltpu.make_async_copy(asend.at[k, pl.ds(s * 6, 6)], out.at[:, out_rows(k), :], self_sem.at[k])

    def direct(k):
        for kind in range(4):
            z_copy(kind, k).start()
        x_copy(0, k).start()

    def forward(k):
        for kind in (2, 3, 0, 1):
            z_arrival(kind, k).wait()
            if kind >= 2:
                z_copy(kind + 3, k).start()
            x_copy({2: 1, 3: 2, 0: 3, 1: 4}[kind], k).start()
        z_copy(4, k).start()

    def last(k):
        for kind, j in ((5, 5), (6, 6), (4, 7)):
            z_arrival(kind, k).wait()
            x_copy(j, k).start()

    def transform(k):
        for j in range(8):
            x_arrival(j, k).wait()
        leg_copy(k).wait()
        row = lax.broadcasted_iota(jnp.int32, (ROWS, 128), 0)
        upper = lax.broadcasted_iota(jnp.int32, (8, QUAD * FIELDS), 0) < 4
        for i in range(GROUPS):
            for j in range(8):
                start = j * 2 * 44
                for band, place in ((2 * j, start), (2 * j + 1, start + MAIN + 8)):
                    natural[pl.ds(place, MAIN), :] = held[band, k, pl.ds(i * MAIN, MAIN), :]
                tails = [held[band, k, pl.ds(2 * MAIN, 8), :].astype(jnp.float32) for band in (2 * j, 2 * j + 1)]
                if i == 0:
                    shared = jnp.where(upper, tails[0], tails[1])
                else:
                    shared = pltpu.roll(jnp.where(upper, tails[1], tails[0]), 4, 0)
                natural[pl.ds(start + MAIN, 8), :] = shared.astype(jnp.bfloat16)
            turned[...] = natural[...].T

            def pair(n, carry, i=i):
                q = (k * GROUPS + i) * QUAD + n
                first, total = first_ref[q], total_ref[q]
                values = leg[q]
                zero = jnp.zeros_like(values)
                low = jnp.where(row < first, values, zero)
                high = jnp.where((row >= first) & (row < total), values, zero)
                fields = turned[pl.ds(pl.multiple_of(n * FIELDS, FIELDS), FIELDS), :]
                sums = jnp.dot(
                    fields, jnp.concatenate([low, high], 1), preferred_element_type=jnp.float32
                )
                slot = i * (2 * QUAD) + 2 * n
                stage[pl.ds(slot, FIELDS, stride=SLOTS), :] = sums[:, :128]
                stage[pl.ds(slot + 1, FIELDS, stride=SLOTS), :] = sums[:, 128:]
                return carry

            lax.fori_loop(0, QUAD, pair, 0)
        esend[k] = stage[...].astype(jnp.bfloat16).reshape(esend.shape[1:])
        for j in range(PIECES):
            e_copy(k, piece_of(j)).start()

    def piece_of(j):
        return lax.rem(s // 4 + 1 + j, PIECES)

    def combine(k):
        sign = jnp.where(parity == 0, 1.0, -1.0).astype(jnp.float32)
        lane = lax.broadcasted_iota(jnp.int32, esend.shape[2:], 2)

        def part(j, carry):
            piece = piece_of(j)
            e_copy(k, piece).wait_recv()
            grid = erecv[k, piece].astype(jnp.float32) + sign * esend[k, piece].astype(jnp.float32)
            columns = pl.ds(piece * (FIELDS // PIECES), FIELDS // PIECES)
            asend[k, columns] = jnp.where(lane < rows_ref[0], grid, 0.0).astype(jnp.bfloat16)

            def send(d, carry):
                t = piece * 4 + lax.rem(s + d, 4)

                @pl.when(t != s)
                def _():
                    pltpu.make_async_remote_copy(
                        src_ref=asend.at[k, pl.ds(t * 6, 6)],
                        dst_ref=out.at[:, out_rows(k), :],
                        send_sem=a_send,
                        recv_sem=a_recv,
                        device_id=(t, b),
                        device_id_type=MESH,
                    ).start()

                @pl.when(t == s)
                def _():
                    self_copy(k).start()

                return carry

            return lax.fori_loop(0, 4, send, carry)

        lax.fori_loop(0, PIECES, part, 0)

    own_copy.wait()

    def begin(k, carry):
        direct(k)
        return carry

    lax.fori_loop(0, 1, begin, 0)

    def step(i, carry):
        @pl.when(i + 1 < CHUNKS)
        def _():
            direct(i + 1)

        for delay, stage_of in ((0, forward), (1, last), (2, transform), (3, combine)):
            k = i - delay

            @pl.when((k >= 0) & (k < CHUNKS))
            def _(k=k, stage_of=stage_of):
                stage_of(k)

        return carry

    lax.fori_loop(0, CHUNKS + 3, step, 0)

    def finish(k, carry):
        for kind in range(7):
            z_copy(kind, k).wait_send()
        for j in range(8):
            x_copy(j, k).wait_send()
        for j in range(PIECES):
            e_copy(k, j).wait_send()
        self_copy(k).wait()
        return carry

    lax.fori_loop(0, CHUNKS, finish, 0)
    sent = asend.at[:, pl.ds(0, 90)]
    pltpu.make_async_copy(sent, sent, a_send).wait()
    got = out.at[:, pl.ds(0, 15 * CHUNKS * SLOTS), :]
    pltpu.make_async_copy(got, got, a_recv).wait()


def shards(coeffs, legendre, wavenumber, band_rows):
    band = lax.axis_index("band")
    parity = band % 2
    first = jnp.maximum((TRUNC - wavenumber - parity) // 2 + 1, 0)
    total = first + jnp.maximum((wavenumber - parity) // 2 + 1, 0)
    split = coeffs.reshape(2, 44, CHUNKS, GROUPS, QUAD * FIELDS)
    main = jnp.where(parity == 0, split[:, :MAIN], split[:, 4:])
    tail = jnp.where(parity == 0, split[:, MAIN:], split[:, :4, :, ::-1])
    cin = jnp.concatenate(
        [part.transpose(0, 2, 3, 1, 4).reshape(2, CHUNKS, -1, QUAD * FIELDS) for part in (main, tail)], 2
    )
    vmem = pl.BlockSpec(memory_space=pltpu.VMEM)
    smem = pl.BlockSpec(memory_space=pltpu.SMEM)
    anywhere = pl.BlockSpec(memory_space=pl.ANY)
    dma = pltpu.SemaphoreType.DMA
    sums = (CHUNKS, PIECES, FIELDS // PIECES, SLOTS, 128)
    return pl.pallas_call(
        kernel,
        out_shape=jax.ShapeDtypeStruct((6, 16 * CHUNKS * SLOTS, 128), jnp.bfloat16),
        in_specs=[vmem, smem, smem, smem, anywhere],
        out_specs=anywhere,
        scratch_shapes=[
            pltpu.VMEM((16, CHUNKS, BLOCK, QUAD * FIELDS), jnp.bfloat16),
            pltpu.VMEM(legendre.shape, jnp.bfloat16),
            pltpu.VMEM((ROWS, QUAD * FIELDS), jnp.bfloat16),
            pltpu.VMEM((QUAD * FIELDS, ROWS), jnp.bfloat16),
            pltpu.VMEM((FIELDS * SLOTS, 128), jnp.float32),
            pltpu.VMEM(sums, jnp.bfloat16),
            pltpu.VMEM(sums, jnp.bfloat16),
            pltpu.VMEM((CHUNKS, FIELDS, SLOTS, 128), jnp.bfloat16),
            dma((CHUNKS,)),
            dma,
            dma((7, CHUNKS)),
            dma((7, CHUNKS)),
            dma((8, CHUNKS)),
            dma((8, CHUNKS)),
            dma((CHUNKS, PIECES)),
            dma((CHUNKS, PIECES)),
            dma,
            dma,
            dma((CHUNKS,)),
        ],
        compiler_params=pltpu.CompilerParams(
            collective_id=0, has_side_effects=True, vmem_limit_bytes=48 * 1024 * 1024
        ),
        cost_estimate=pl.CostEstimate(
            flops=2 * 40 * ROWS * 96 * 256, bytes_accessed=20_000_000, transcendentals=0
        ),
    )(cin, first, total, band_rows, legendre)


def solution(mesh):
    in_specs = (P(None, "band", "mset"), P("mset", None, "band"), P("mset"), P("band"))
    out_specs = P("mset", None, "band")
    return jax.shard_map(shards, mesh=mesh, in_specs=in_specs, out_specs=out_specs, check_vma=False)
```

```python
import jax
import jax.numpy as jnp
from jax import lax
from jax.experimental import pallas as pl
from jax.experimental.pallas import tpu as pltpu
from jax.sharding import PartitionSpec as P

TRUNC = 1279
MESH = pl.DeviceIdType.MESH
CHUNKS = 5
GROUPS = 2
QUAD = 4
FIELDS = 96
ROWS = 704
MAIN = 40
BLOCK = 2 * MAIN + 8
SLOTS = 2 * GROUPS * QUAD
PIECES = 8
PEERS = 16 // PIECES
OFFSETS = (0, -1, 1, -2, 2, -3, 3, 4)


def kernel(
    coeffs, wave_ref, rows_ref, legendre, out,
    raw, other, held, leg, natural, turned, stage, esend, erecv, asend,
    leg_sem, raw_sem, z_send, z_recv, x_send, x_recv, e_send, e_recv, a_send, a_recv, self_sem,
):
    s = lax.axis_index("mset")
    b = lax.axis_index("band")
    xl, z = b // 8, b % 8
    parity = z % 2

    def at_z(offset):
        return lax.rem(z + (8 + offset), 8)

    def on_line(offset):
        return (s, xl * 8 + at_z(offset))

    def own_slot(offset):
        return xl * 8 + at_z(offset)

    across = (s, (1 - xl) * 8 + z)
    mirror = (s, xl * 8 + z + 1 - 2 * parity)

    barrier = pltpu.get_barrier_semaphore()
    for device in (on_line(-2), on_line(-1), on_line(1), on_line(2), across):
        pl.semaphore_signal(barrier, inc=1, device_id=device, device_id_type=MESH)

    def greet(d, carry):
        pl.semaphore_signal(barrier, inc=1, device_id=(lax.rem(s + d, 16), b), device_id_type=MESH)
        return carry

    lax.fori_loop(1, 16, greet, 0)

    def leg_copy(k):
        pairs = pl.ds(k * GROUPS * QUAD, GROUPS * QUAD)
        return pltpu.make_async_copy(legendre.at[pairs], leg.at[pairs], leg_sem.at[k])

    raw_copy = pltpu.make_async_copy(coeffs, raw, raw_sem)
    raw_copy.start()
    for k in range(CHUNKS):
        leg_copy(k).start()
    raw_copy.wait()

    def pack(k):
        both = []
        for i in range(GROUPS):
            start = pl.multiple_of((k * GROUPS + i) * (QUAD * FIELDS), QUAD * FIELDS)
            both.append(raw[:, :, pl.ds(start, QUAD * FIELDS)].astype(jnp.float32))

        def fill(put, p):
            parts = [values[:, p, :] for values in both]
            if parity_of == 0:
                mains, tails = [v[:MAIN] for v in parts], [v[MAIN:] for v in parts]
            else:
                mains, tails = [v[4:] for v in parts], [v[:4] for v in reversed(parts)]
            put(0, mains[0])
            put(MAIN, mains[1])
            put(2 * MAIN, jnp.concatenate(tails, 0))

        def put_own(row, values):
            held[own_slot(0), k, pl.ds(row, values.shape[0]), :] = values.astype(jnp.bfloat16)

        def put_other(row, values):
            other[k, pl.ds(row, values.shape[0]), :] = values.astype(jnp.bfloat16)

        for parity_of in range(2):

            @pl.when(parity == parity_of)
            def _():
                fill(put_own, parity_of)
                fill(put_other, 1 - parity_of)

    pack(0)
    pl.semaphore_wait(barrier, 20)

    def z_copy(kind, k):
        if kind == 4:
            way = 1 - 2 * lax.rem(k + s, 2)
            block, target = -2 * way, 2 * way
        else:
            block, target = {0: (0, 2), 1: (0, -2), 2: (0, 1), 3: (0, -1), 5: (-1, 2), 6: (1, -2)}[kind]
        src = other.at[k] if kind in (2, 3) else held.at[own_slot(block), k]
        return pltpu.make_async_remote_copy(
            src_ref=src,
            dst_ref=held.at[own_slot(block), k],
            send_sem=z_send.at[kind, k],
            recv_sem=z_recv.at[kind, k],
            device_id=on_line(target),
            device_id_type=MESH,
        )

    def z_arrival(kind, k):
        block = {0: -2, 1: 2, 2: -1, 3: 1, 4: 4, 5: -3, 6: 3}[kind]
        here = held.at[own_slot(block), k]
        return pltpu.make_async_copy(here, here, z_recv.at[kind, k])

    def x_copy(j, k):
        slot = own_slot(OFFSETS[j])
        return pltpu.make_async_remote_copy(
            src_ref=held.at[slot, k],
            dst_ref=held.at[slot, k],
            send_sem=x_send.at[j, k],
            recv_sem=x_recv.at[j, k],
            device_id=across,
            device_id_type=MESH,
        )

    def x_arrival(j, k):
        here = held.at[(1 - xl) * 8 + at_z(OFFSETS[j]), k]
        return pltpu.make_async_copy(here, here, x_recv.at[j, k])

    def e_copy(k, piece):
        return pltpu.make_async_remote_copy(
            src_ref=esend.at[k, piece],
            dst_ref=erecv.at[k, piece],
            send_sem=e_send.at[k, piece],
            recv_sem=e_recv.at[k, piece],
            device_id=mirror,
            device_id_type=MESH,
        )

    def out_rows(k):
        return pl.ds(pl.multiple_of(s * (CHUNKS * SLOTS) + k * SLOTS, SLOTS), SLOTS)

    def self_copy(k):
        return pltpu.make_async_copy(asend.at[k, pl.ds(s * 6, 6)], out.at[:, out_rows(k), :], self_sem.at[k])

    def direct(k):
        for kind in range(4):
            z_copy(kind, k).start()
        x_copy(0, k).start()

    def forward(k):
        for kind in (2, 3, 0, 1):
            z_arrival(kind, k).wait()
            if kind >= 2:
                z_copy(kind + 3, k).start()
            x_copy({2: 1, 3: 2, 0: 3, 1: 4}[kind], k).start()
        z_copy(4, k).start()

    def last(k):
        for kind, j in ((5, 5), (6, 6), (4, 7)):
            z_arrival(kind, k).wait()
            x_copy(j, k).start()

    def transform(k):
        for j in range(8):
            x_arrival(j, k).wait()
        leg_copy(k).wait()
        row = lax.broadcasted_iota(jnp.int32, (ROWS, 128), 0)
        upper = lax.broadcasted_iota(jnp.int32, (8, QUAD * FIELDS), 0) < 4
        for i in range(GROUPS):
            for j in range(8):
                start = j * 2 * 44
                for band, place in ((2 * j, start), (2 * j + 1, start + MAIN + 8)):
                    natural[pl.ds(place, MAIN), :] = held[band, k, pl.ds(i * MAIN, MAIN), :]
                tails = [held[band, k, pl.ds(2 * MAIN, 8), :].astype(jnp.float32) for band in (2 * j, 2 * j + 1)]
                if i == 0:
                    shared = jnp.where(upper, tails[0], tails[1])
                else:
                    shared = pltpu.roll(jnp.where(upper, tails[1], tails[0]), 4, 0)
                natural[pl.ds(start + MAIN, 8), :] = shared.astype(jnp.bfloat16)
            turned[...] = natural[...].T

            def pair(n, carry, i=i):
                q = (k * GROUPS + i) * QUAD + n
                m = wave_ref[q]
                first = jnp.maximum(lax.shift_right_arithmetic(TRUNC - m - parity, 1) + 1, 0)
                total = first + jnp.maximum(lax.shift_right_arithmetic(m - parity, 1) + 1, 0)
                values = leg[q]
                zero = jnp.zeros_like(values)
                low = jnp.where(row < first, values, zero)
                high = jnp.where((row >= first) & (row < total), values, zero)
                fields = turned[pl.ds(pl.multiple_of(n * FIELDS, FIELDS), FIELDS), :]
                sums = jnp.dot(
                    fields, jnp.concatenate([low, high], 1), preferred_element_type=jnp.float32
                )
                slot = i * (2 * QUAD) + 2 * n
                stage[pl.ds(slot, FIELDS, stride=SLOTS), :] = sums[:, :128]
                stage[pl.ds(slot + 1, FIELDS, stride=SLOTS), :] = sums[:, 128:]
                return carry

            lax.fori_loop(0, QUAD, pair, 0)
        esend[k] = stage[...].astype(jnp.bfloat16).reshape(esend.shape[1:])
        for j in range(PIECES):
            e_copy(k, piece_of(j)).start()

    def piece_of(j):
        return lax.rem(s // PEERS + 1 + j, PIECES)

    def combine(k):
        sign = jnp.where(parity == 0, 1.0, -1.0).astype(jnp.float32)
        lane = lax.broadcasted_iota(jnp.int32, esend.shape[2:], 2)

        def part(j, carry):
            piece = piece_of(j)
            e_copy(k, piece).wait_recv()
            grid = erecv[k, piece].astype(jnp.float32) + sign * esend[k, piece].astype(jnp.float32)
            columns = pl.ds(piece * (FIELDS // PIECES), FIELDS // PIECES)
            asend[k, columns] = jnp.where(lane < rows_ref[0], grid, 0.0).astype(jnp.bfloat16)

            def send(d, carry):
                t = piece * PEERS + lax.rem(s + 1 + d, PEERS)

                @pl.when(t != s)
                def _():
                    pltpu.make_async_remote_copy(
                        src_ref=asend.at[k, pl.ds(t * 6, 6)],
                        dst_ref=out.at[:, out_rows(k), :],
                        send_sem=a_send,
                        recv_sem=a_recv,
                        device_id=(t, b),
                        device_id_type=MESH,
                    ).start()

                @pl.when(t == s)
                def _():
                    self_copy(k).start()

                return carry

            return lax.fori_loop(0, PEERS, send, carry)

        lax.fori_loop(0, PIECES, part, 0)

    direct(0)

    def drain(k):
        for kind in range(7):
            z_copy(kind, k).wait_send()
        for j in range(8):
            x_copy(j, k).wait_send()

    def step(i, carry):
        @pl.when(i + 1 < CHUNKS)
        def _():
            pack(i + 1)
            direct(i + 1)

        for delay, stage_of in ((0, forward), (1, last), (2, transform), (3, drain), (3, combine)):
            k = i - delay

            @pl.when((k >= 0) & (k < CHUNKS))
            def _(k=k, stage_of=stage_of):
                stage_of(k)

        return carry

    lax.fori_loop(0, CHUNKS + 3, step, 0)

    def finish(k, carry):
        for j in range(PIECES):
            e_copy(k, j).wait_send()
        self_copy(k).wait()
        return carry

    lax.fori_loop(0, CHUNKS, finish, 0)
    sent = asend.at[:, pl.ds(0, 90)]
    pltpu.make_async_copy(sent, sent, a_send).wait()
    got = out.at[:, pl.ds(0, 15 * CHUNKS * SLOTS), :]
    pltpu.make_async_copy(got, got, a_recv).wait()


def shards(coeffs, legendre, wavenumber, band_rows):
    smem = pl.BlockSpec(memory_space=pltpu.SMEM)
    anywhere = pl.BlockSpec(memory_space=pl.ANY)
    dma = pltpu.SemaphoreType.DMA
    sums = (CHUNKS, PIECES, FIELDS // PIECES, SLOTS, 128)
    return pl.pallas_call(
        kernel,
        out_shape=jax.ShapeDtypeStruct((6, 16 * CHUNKS * SLOTS, 128), jnp.bfloat16),
        in_specs=[anywhere, smem, smem, anywhere],
        out_specs=anywhere,
        scratch_shapes=[
            pltpu.VMEM((44, 2, coeffs.shape[2]), jnp.bfloat16),
            pltpu.VMEM((CHUNKS, BLOCK, QUAD * FIELDS), jnp.bfloat16),
            pltpu.VMEM((16, CHUNKS, BLOCK, QUAD * FIELDS), jnp.bfloat16),
            pltpu.VMEM(legendre.shape, jnp.bfloat16),
            pltpu.VMEM((ROWS, QUAD * FIELDS), jnp.bfloat16),
            pltpu.VMEM((QUAD * FIELDS, ROWS), jnp.bfloat16),
            pltpu.VMEM((FIELDS * SLOTS, 128), jnp.float32),
            pltpu.VMEM(sums, jnp.bfloat16),
            pltpu.VMEM(sums, jnp.bfloat16),
            pltpu.VMEM((CHUNKS, FIELDS, SLOTS, 128), jnp.bfloat16),
            dma((CHUNKS,)),
            dma,
            dma((7, CHUNKS)),
            dma((7, CHUNKS)),
            dma((8, CHUNKS)),
            dma((8, CHUNKS)),
            dma((CHUNKS, PIECES)),
            dma((CHUNKS, PIECES)),
            dma,
            dma,
            dma((CHUNKS,)),
        ],
        compiler_params=pltpu.CompilerParams(
            collective_id=0, has_side_effects=True, vmem_limit_bytes=48 * 1024 * 1024
        ),
        cost_estimate=pl.CostEstimate(
            flops=2 * 40 * ROWS * 96 * 256, bytes_accessed=20_000_000, transcendentals=0
        ),
    )(jnp.swapaxes(coeffs, 0, 1), wavenumber, band_rows, legendre)


def solution(mesh):
    in_specs = (P(None, "band", "mset"), P("mset", None, "band"), P("mset"), P("band"))
    out_specs = P("mset", None, "band")
    return jax.shard_map(shards, mesh=mesh, in_specs=in_specs, out_specs=out_specs, check_vma=False)
```

```python
import jax
import jax.numpy as jnp
from jax import lax
from jax.experimental import pallas as pl
from jax.experimental.pallas import tpu as pltpu
from jax.sharding import PartitionSpec as P

TRUNC = 1279
MESH = pl.DeviceIdType.MESH
CHUNKS = 5
GROUPS = 2
QUAD = 4
FIELDS = 96
ROWS = 704
MAIN = 40
BLOCK = 2 * MAIN + 8
SLOTS = 2 * GROUPS * QUAD
PIECES = 8
PEERS = 16 // PIECES
OFFSETS = (0, -1, 1, -2, 2, -3, 3, 4)


def kernel(
    coeffs, wavenumber, band_rows, legendre, out,
    wave_ref, rows_ref, raw, other, held, leg, natural, turned, stage, esend, erecv, asend,
    leg_sem, raw_sem, small_sem, z_send, z_recv, x_send, x_recv, e_send, e_recv, a_send, a_recv, self_sem,
):
    s = lax.axis_index("mset")
    b = lax.axis_index("band")
    xl, z = b // 8, b % 8
    parity = z % 2

    def at_z(offset):
        return lax.rem(z + (8 + offset), 8)

    def on_line(offset):
        return (s, xl * 8 + at_z(offset))

    def own_slot(offset):
        return xl * 8 + at_z(offset)

    across = (s, (1 - xl) * 8 + z)
    mirror = (s, xl * 8 + z + 1 - 2 * parity)

    barrier = pltpu.get_barrier_semaphore()
    for device in (on_line(-2), on_line(-1), on_line(1), on_line(2), across):
        pl.semaphore_signal(barrier, inc=1, device_id=device, device_id_type=MESH)

    def greet(d, carry):
        pl.semaphore_signal(barrier, inc=1, device_id=(lax.rem(s + d, 16), b), device_id_type=MESH)
        return carry

    lax.fori_loop(1, 16, greet, 0)

    def leg_copy(k):
        pairs = pl.ds(k * GROUPS * QUAD, GROUPS * QUAD)
        return pltpu.make_async_copy(legendre.at[pairs], leg.at[pairs], leg_sem.at[k])

    raw_copy = pltpu.make_async_copy(coeffs, raw, raw_sem)
    raw_copy.start()
    small_copies = [
        pltpu.make_async_copy(src, dst, small_sem.at[i])
        for i, (src, dst) in enumerate(((wavenumber, wave_ref), (band_rows, rows_ref)))
    ]
    for copy in small_copies:
        copy.start()
    for k in range(CHUNKS):
        leg_copy(k).start()
    raw_copy.wait()
    for copy in small_copies:
        copy.wait()

    def pack(k):
        both = []
        for i in range(GROUPS):
            start = pl.multiple_of((k * GROUPS + i) * (QUAD * FIELDS), QUAD * FIELDS)
            both.append(raw[:, :, pl.ds(start, QUAD * FIELDS)].astype(jnp.float32))

        def fill(put, p):
            parts = [values[:, p, :] for values in both]
            if parity_of == 0:
                mains, tails = [v[:MAIN] for v in parts], [v[MAIN:] for v in parts]
            else:
                mains, tails = [v[4:] for v in parts], [v[:4] for v in reversed(parts)]
            put(0, mains[0])
            put(MAIN, mains[1])
            put(2 * MAIN, jnp.concatenate(tails, 0))

        def put_own(row, values):
            held[own_slot(0), k, pl.ds(row, values.shape[0]), :] = values.astype(jnp.bfloat16)

        def put_other(row, values):
            other[k, pl.ds(row, values.shape[0]), :] = values.astype(jnp.bfloat16)

        for parity_of in range(2):

            @pl.when(parity == parity_of)
            def _():
                fill(put_own, parity_of)
                fill(put_other, 1 - parity_of)

    pack(0)
    pl.semaphore_wait(barrier, 20)

    def z_copy(kind, k):
        if kind == 4:
            way = 1 - 2 * lax.rem(k + s, 2)
            block, target = -2 * way, 2 * way
        else:
            block, target = {0: (0, 2), 1: (0, -2), 2: (0, 1), 3: (0, -1), 5: (-1, 2), 6: (1, -2)}[kind]
        src = other.at[k] if kind in (2, 3) else held.at[own_slot(block), k]
        return pltpu.make_async_remote_copy(
            src_ref=src,
            dst_ref=held.at[own_slot(block), k],
            send_sem=z_send.at[kind, k],
            recv_sem=z_recv.at[kind, k],
            device_id=on_line(target),
            device_id_type=MESH,
        )

    def z_arrival(kind, k):
        block = {0: -2, 1: 2, 2: -1, 3: 1, 4: 4, 5: -3, 6: 3}[kind]
        here = held.at[own_slot(block), k]
        return pltpu.make_async_copy(here, here, z_recv.at[kind, k])

    def x_copy(j, k):
        slot = own_slot(OFFSETS[j])
        return pltpu.make_async_remote_copy(
            src_ref=held.at[slot, k],
            dst_ref=held.at[slot, k],
            send_sem=x_send.at[j, k],
            recv_sem=x_recv.at[j, k],
            device_id=across,
            device_id_type=MESH,
        )

    def x_arrival(j, k):
        here = held.at[(1 - xl) * 8 + at_z(OFFSETS[j]), k]
        return pltpu.make_async_copy(here, here, x_recv.at[j, k])

    def e_copy(k, piece):
        return pltpu.make_async_remote_copy(
            src_ref=esend.at[k, piece],
            dst_ref=erecv.at[k, piece],
            send_sem=e_send.at[k, piece],
            recv_sem=e_recv.at[k, piece],
            device_id=mirror,
            device_id_type=MESH,
        )

    def out_rows(k):
        return pl.ds(pl.multiple_of(s * (CHUNKS * SLOTS) + k * SLOTS, SLOTS), SLOTS)

    def self_copy(k):
        return pltpu.make_async_copy(asend.at[k, pl.ds(s * 6, 6)], out.at[:, out_rows(k), :], self_sem.at[k])

    def direct(k):
        for kind in range(4):
            z_copy(kind, k).start()
        x_copy(0, k).start()

    def forward(k):
        for kind in (2, 3, 0, 1):
            z_arrival(kind, k).wait()
            if kind >= 2:
                z_copy(kind + 3, k).start()
            x_copy({2: 1, 3: 2, 0: 3, 1: 4}[kind], k).start()
        z_copy(4, k).start()

    def last(k):
        for kind, j in ((5, 5), (6, 6), (4, 7)):
            z_arrival(kind, k).wait()
            x_copy(j, k).start()

    def transform(k):
        for j in range(8):
            x_arrival(j, k).wait()
        leg_copy(k).wait()
        row = lax.broadcasted_iota(jnp.int32, (ROWS, 128), 0)
        upper = lax.broadcasted_iota(jnp.int32, (8, QUAD * FIELDS), 0) < 4
        for i in range(GROUPS):
            for j in range(8):
                start = j * 2 * 44
                for band, place in ((2 * j, start), (2 * j + 1, start + MAIN + 8)):
                    natural[pl.ds(place, MAIN), :] = held[band, k, pl.ds(i * MAIN, MAIN), :]
                tails = [held[band, k, pl.ds(2 * MAIN, 8), :].astype(jnp.float32) for band in (2 * j, 2 * j + 1)]
                if i == 0:
                    shared = jnp.where(upper, tails[0], tails[1])
                else:
                    shared = pltpu.roll(jnp.where(upper, tails[1], tails[0]), 4, 0)
                natural[pl.ds(start + MAIN, 8), :] = shared.astype(jnp.bfloat16)
            turned[...] = natural[...].T

            def pair(n, carry, i=i):
                q = (k * GROUPS + i) * QUAD + n
                m = wave_ref[q]
                first = jnp.maximum(lax.shift_right_arithmetic(TRUNC - m - parity, 1) + 1, 0)
                total = first + jnp.maximum(lax.shift_right_arithmetic(m - parity, 1) + 1, 0)
                values = leg[q]
                zero = jnp.zeros_like(values)
                low = jnp.where(row < first, values, zero)
                high = jnp.where((row >= first) & (row < total), values, zero)
                fields = turned[pl.ds(pl.multiple_of(n * FIELDS, FIELDS), FIELDS), :]
                sums = jnp.dot(
                    fields, jnp.concatenate([low, high], 1), preferred_element_type=jnp.float32
                )
                slot = i * (2 * QUAD) + 2 * n
                stage[pl.ds(slot, FIELDS, stride=SLOTS), :] = sums[:, :128]
                stage[pl.ds(slot + 1, FIELDS, stride=SLOTS), :] = sums[:, 128:]
                return carry

            lax.fori_loop(0, QUAD, pair, 0)
        esend[k] = stage[...].astype(jnp.bfloat16).reshape(esend.shape[1:])
        for j in range(PIECES):
            e_copy(k, piece_of(j)).start()

    def piece_of(j):
        return lax.rem(s // PEERS + 1 + j, PIECES)

    def combine(k):
        sign = jnp.where(parity == 0, 1.0, -1.0).astype(jnp.float32)
        lane = lax.broadcasted_iota(jnp.int32, esend.shape[2:], 2)

        def part(j, carry):
            piece = piece_of(j)
            e_copy(k, piece).wait_recv()
            grid = erecv[k, piece].astype(jnp.float32) + sign * esend[k, piece].astype(jnp.float32)
            columns = pl.ds(piece * (FIELDS // PIECES), FIELDS // PIECES)
            asend[k, columns] = jnp.where(lane < rows_ref[0], grid, 0.0).astype(jnp.bfloat16)

            def send(d, carry):
                t = piece * PEERS + lax.rem(s + 1 + d, PEERS)

                @pl.when(t != s)
                def _():
                    pltpu.make_async_remote_copy(
                        src_ref=asend.at[k, pl.ds(t * 6, 6)],
                        dst_ref=out.at[:, out_rows(k), :],
                        send_sem=a_send,
                        recv_sem=a_recv,
                        device_id=(t, b),
                        device_id_type=MESH,
                    ).start()

                @pl.when(t == s)
                def _():
                    self_copy(k).start()

                return carry

            return lax.fori_loop(0, PEERS, send, carry)

        lax.fori_loop(0, PIECES, part, 0)

    direct(0)

    def drain(k):
        for kind in range(7):
            z_copy(kind, k).wait_send()
        for j in range(8):
            x_copy(j, k).wait_send()

    def step(i, carry):
        @pl.when(i + 1 < CHUNKS)
        def _():
            pack(i + 1)
            direct(i + 1)

        for delay, stage_of in ((0, forward), (1, last), (2, transform), (3, drain), (3, combine)):
            k = i - delay

            @pl.when((k >= 0) & (k < CHUNKS))
            def _(k=k, stage_of=stage_of):
                stage_of(k)

        return carry

    lax.fori_loop(0, CHUNKS + 3, step, 0)

    def finish(k, carry):
        for j in range(PIECES):
            e_copy(k, j).wait_send()
        self_copy(k).wait()
        return carry

    lax.fori_loop(0, CHUNKS, finish, 0)
    sent = asend.at[:, pl.ds(0, 90)]
    pltpu.make_async_copy(sent, sent, a_send).wait()
    got = out.at[:, pl.ds(0, 15 * CHUNKS * SLOTS), :]
    pltpu.make_async_copy(got, got, a_recv).wait()


def shards(coeffs, legendre, wavenumber, band_rows):
    hbm = pl.BlockSpec(memory_space=pltpu.HBM)
    anywhere = pl.BlockSpec(memory_space=pl.ANY)
    dma = pltpu.SemaphoreType.DMA
    sums = (CHUNKS, PIECES, FIELDS // PIECES, SLOTS, 128)
    return pl.pallas_call(
        kernel,
        out_shape=jax.ShapeDtypeStruct((6, 16 * CHUNKS * SLOTS, 128), jnp.bfloat16),
        in_specs=[hbm, hbm, hbm, hbm],
        out_specs=anywhere,
        scratch_shapes=[
            pltpu.SMEM(wavenumber.shape, jnp.int32),
            pltpu.SMEM(band_rows.shape, jnp.int32),
            pltpu.VMEM((44, 2, coeffs.shape[2]), jnp.bfloat16),
            pltpu.VMEM((CHUNKS, BLOCK, QUAD * FIELDS), jnp.bfloat16),
            pltpu.VMEM((16, CHUNKS, BLOCK, QUAD * FIELDS), jnp.bfloat16),
            pltpu.VMEM(legendre.shape, jnp.bfloat16),
            pltpu.VMEM((ROWS, QUAD * FIELDS), jnp.bfloat16),
            pltpu.VMEM((QUAD * FIELDS, ROWS), jnp.bfloat16),
            pltpu.VMEM((FIELDS * SLOTS, 128), jnp.float32),
            pltpu.VMEM(sums, jnp.bfloat16),
            pltpu.VMEM(sums, jnp.bfloat16),
            pltpu.VMEM((CHUNKS, FIELDS, SLOTS, 128), jnp.bfloat16),
            dma((CHUNKS,)),
            dma,
            dma((2,)),
            dma((7, CHUNKS)),
            dma((7, CHUNKS)),
            dma((8, CHUNKS)),
            dma((8, CHUNKS)),
            dma((CHUNKS, PIECES)),
            dma((CHUNKS, PIECES)),
            dma,
            dma,
            dma((CHUNKS,)),
        ],
        compiler_params=pltpu.CompilerParams(
            collective_id=0, has_side_effects=True, vmem_limit_bytes=48 * 1024 * 1024
        ),
        cost_estimate=pl.CostEstimate(
            flops=2 * 40 * ROWS * 96 * 256, bytes_accessed=20_000_000, transcendentals=0
        ),
    )(pltpu.with_memory_space_constraint(jnp.swapaxes(coeffs, 0, 1), pltpu.HBM), pltpu.with_memory_space_constraint(wavenumber, pltpu.HBM), band_rows, legendre)


def solution(mesh):
    in_specs = (P(None, "band", "mset"), P("mset", None, "band"), P("mset"), P("band"))
    out_specs = P("mset", None, "band")
    return jax.shard_map(shards, mesh=mesh, in_specs=in_specs, out_specs=out_specs, check_vma=False)
```

```python
import jax
import jax.numpy as jnp
from jax import lax
from jax.experimental import pallas as pl
from jax.experimental.pallas import tpu as pltpu
from jax.sharding import PartitionSpec as P

TRUNC = 1279
MESH = pl.DeviceIdType.MESH
CHUNKS = 5
GROUPS = 2
QUAD = 4
FIELDS = 96
ROWS = 704
MAIN = 40
BLOCK = 2 * MAIN + 8
SLOTS = 2 * GROUPS * QUAD
PIECES = 8
PEERS = 16 // PIECES
OFFSETS = (0, -1, 1, -2, 2, -3, 3, 4)


def kernel(
    coeffs, wavenumber, band_rows, legendre, out,
    wave_ref, rows_ref, raw, other, held, leg, natural, turned, stage, esend, erecv, asend,
    leg_sem, raw_sem, small_sem, z_send, z_recv, x_send, x_recv, e_send, e_recv, a_send, a_recv, self_sem,
):
    s = lax.axis_index("mset")
    b = lax.axis_index("band")
    xl, z = b // 8, b % 8
    parity = z % 2

    def at_z(offset):
        return lax.rem(z + (8 + offset), 8)

    def on_line(offset):
        return (s, xl * 8 + at_z(offset))

    def own_slot(offset):
        return xl * 8 + at_z(offset)

    across = (s, (1 - xl) * 8 + z)
    mirror = (s, xl * 8 + z + 1 - 2 * parity)

    barrier = pltpu.get_barrier_semaphore()
    for device in (on_line(-2), on_line(-1), on_line(1), on_line(2), across):
        pl.semaphore_signal(barrier, inc=1, device_id=device, device_id_type=MESH)

    def greet(d, carry):
        pl.semaphore_signal(barrier, inc=1, device_id=(lax.rem(s + d, 16), b), device_id_type=MESH)
        return carry

    lax.fori_loop(1, 16, greet, 0)

    def leg_copy(k):
        pairs = pl.ds(k * GROUPS * QUAD, GROUPS * QUAD)
        return pltpu.make_async_copy(legendre.at[pairs], leg.at[pairs], leg_sem.at[k])

    raw_copy = pltpu.make_async_copy(coeffs, raw, raw_sem)
    raw_copy.start()
    small_copies = [
        pltpu.make_async_copy(src, dst, small_sem.at[i])
        for i, (src, dst) in enumerate(((wavenumber, wave_ref), (band_rows, rows_ref)))
    ]
    for copy in small_copies:
        copy.start()
    for k in range(CHUNKS):
        leg_copy(k).start()
    raw_copy.wait()
    for copy in small_copies:
        copy.wait()

    def pack(k):
        both = []
        for i in range(GROUPS):
            start = pl.multiple_of((k * GROUPS + i) * (QUAD * FIELDS), QUAD * FIELDS)
            both.append(raw[:, :, pl.ds(start, QUAD * FIELDS)].astype(jnp.float32))

        def fill(put, p):
            parts = [values[:, p, :] for values in both]
            if parity_of == 0:
                mains, tails = [v[:MAIN] for v in parts], [v[MAIN:] for v in parts]
            else:
                mains, tails = [v[4:] for v in parts], [v[:4] for v in reversed(parts)]
            put(0, mains[0])
            put(MAIN, mains[1])
            put(2 * MAIN, jnp.concatenate(tails, 0))

        def put_own(row, values):
            held[own_slot(0), k, pl.ds(row, values.shape[0]), :] = values.astype(jnp.bfloat16)

        def put_other(row, values):
            other[k, pl.ds(row, values.shape[0]), :] = values.astype(jnp.bfloat16)

        for parity_of in range(2):

            @pl.when(parity == parity_of)
            def _():
                fill(put_own, parity_of)
                fill(put_other, 1 - parity_of)

    pack(0)
    pl.semaphore_wait(barrier, 20)

    def z_copy(kind, k):
        if kind == 4:
            way = 1 - 2 * lax.rem(k + s, 2)
            block, target = -2 * way, 2 * way
        else:
            block, target = {0: (0, 2), 1: (0, -2), 2: (0, 1), 3: (0, -1), 5: (-1, 2), 6: (1, -2)}[kind]
        src = other.at[k] if kind in (2, 3) else held.at[own_slot(block), k]
        return pltpu.make_async_remote_copy(
            src_ref=src,
            dst_ref=held.at[own_slot(block), k],
            send_sem=z_send.at[kind, k],
            recv_sem=z_recv.at[kind, k],
            device_id=on_line(target),
            device_id_type=MESH,
        )

    def z_arrival(kind, k):
        block = {0: -2, 1: 2, 2: -1, 3: 1, 4: 4, 5: -3, 6: 3}[kind]
        here = held.at[own_slot(block), k]
        return pltpu.make_async_copy(here, here, z_recv.at[kind, k])

    def x_copy(j, k):
        slot = own_slot(OFFSETS[j])
        return pltpu.make_async_remote_copy(
            src_ref=held.at[slot, k],
            dst_ref=held.at[slot, k],
            send_sem=x_send.at[j, k],
            recv_sem=x_recv.at[j, k],
            device_id=across,
            device_id_type=MESH,
        )

    def x_arrival(j, k):
        here = held.at[(1 - xl) * 8 + at_z(OFFSETS[j]), k]
        return pltpu.make_async_copy(here, here, x_recv.at[j, k])

    def e_copy(k, piece):
        return pltpu.make_async_remote_copy(
            src_ref=esend.at[k, piece],
            dst_ref=erecv.at[k, piece],
            send_sem=e_send.at[k, piece],
            recv_sem=e_recv.at[k, piece],
            device_id=mirror,
            device_id_type=MESH,
        )

    def out_rows(k):
        return pl.ds(pl.multiple_of(s * (CHUNKS * SLOTS) + k * SLOTS, SLOTS), SLOTS)

    def self_copy(k):
        return pltpu.make_async_copy(asend.at[k, pl.ds(s * 6, 6)], out.at[:, out_rows(k), :], self_sem.at[k])

    def direct(k):
        for kind in range(4):
            z_copy(kind, k).start()
        x_copy(0, k).start()

    def forward(k):
        for kind in (2, 3, 0, 1):
            z_arrival(kind, k).wait()
            if kind >= 2:
                z_copy(kind + 3, k).start()
            x_copy({2: 1, 3: 2, 0: 3, 1: 4}[kind], k).start()
        z_copy(4, k).start()

    def last(k):
        for kind, j in ((5, 5), (6, 6), (4, 7)):
            z_arrival(kind, k).wait()
            x_copy(j, k).start()

    def transform(k):
        for j in range(8):
            x_arrival(j, k).wait()
        leg_copy(k).wait()
        row = lax.broadcasted_iota(jnp.int32, (ROWS, 128), 0)
        upper = lax.broadcasted_iota(jnp.int32, (8, QUAD * FIELDS), 0) < 4
        for i in range(GROUPS):
            for j in range(8):
                start = j * 2 * 44
                for band, place in ((2 * j, start), (2 * j + 1, start + MAIN + 8)):
                    natural[pl.ds(place, MAIN), :] = held[band, k, pl.ds(i * MAIN, MAIN), :]
                tails = [held[band, k, pl.ds(2 * MAIN, 8), :].astype(jnp.float32) for band in (2 * j, 2 * j + 1)]
                if i == 0:
                    shared = jnp.where(upper, tails[0], tails[1])
                else:
                    shared = pltpu.roll(jnp.where(upper, tails[1], tails[0]), 4, 0)
                natural[pl.ds(start + MAIN, 8), :] = shared.astype(jnp.bfloat16)
            turned[...] = natural[...].T

            def pair(n, carry, i=i):
                q = (k * GROUPS + i) * QUAD + n
                m = wave_ref[q]
                first = jnp.maximum(lax.shift_right_arithmetic(TRUNC - m - parity, 1) + 1, 0)
                total = first + jnp.maximum(lax.shift_right_arithmetic(m - parity, 1) + 1, 0)
                values = leg[q]
                zero = jnp.zeros_like(values)
                low = jnp.where(row < first, values, zero)
                high = jnp.where((row >= first) & (row < total), values, zero)
                fields = turned[pl.ds(pl.multiple_of(n * FIELDS, FIELDS), FIELDS), :]
                sums = jnp.dot(
                    fields, jnp.concatenate([low, high], 1), preferred_element_type=jnp.float32
                )
                slot = i * (2 * QUAD) + 2 * n
                stage[pl.ds(slot, FIELDS, stride=SLOTS), :] = sums[:, :128]
                stage[pl.ds(slot + 1, FIELDS, stride=SLOTS), :] = sums[:, 128:]
                return carry

            lax.fori_loop(0, QUAD, pair, 0)
        esend[k] = stage[...].astype(jnp.bfloat16).reshape(esend.shape[1:])
        for j in range(PIECES):
            e_copy(k, piece_of(j)).start()

    def piece_of(j):
        return lax.rem(s // PEERS + 1 + j, PIECES)

    def combine(k):
        sign = jnp.where(parity == 0, 1.0, -1.0).astype(jnp.float32)
        lane = lax.broadcasted_iota(jnp.int32, esend.shape[2:], 2)

        def part(j, carry):
            piece = piece_of(j)
            e_copy(k, piece).wait_recv()
            grid = erecv[k, piece].astype(jnp.float32) + sign * esend[k, piece].astype(jnp.float32)
            columns = pl.ds(piece * (FIELDS // PIECES), FIELDS // PIECES)
            asend[k, columns] = jnp.where(lane < rows_ref[0], grid, 0.0).astype(jnp.bfloat16)

            def send(d, carry):
                t = piece * PEERS + lax.rem(s + 1 + d, PEERS)

                @pl.when(t != s)
                def _():
                    pltpu.make_async_remote_copy(
                        src_ref=asend.at[k, pl.ds(t * 6, 6)],
                        dst_ref=out.at[:, out_rows(k), :],
                        send_sem=a_send,
                        recv_sem=a_recv,
                        device_id=(t, b),
                        device_id_type=MESH,
                    ).start()

                @pl.when(t == s)
                def _():
                    self_copy(k).start()

                return carry

            return lax.fori_loop(0, PEERS, send, carry)

        lax.fori_loop(0, PIECES, part, 0)

    direct(0)

    def drain(k):
        for kind in range(7):
            z_copy(kind, k).wait_send()
        for j in range(8):
            x_copy(j, k).wait_send()

    def step(i, carry):
        @pl.when(i + 1 < CHUNKS)
        def _():
            pack(i + 1)
            direct(i + 1)

        for delay, stage_of in ((0, forward), (1, last), (2, transform), (4, drain), (4, combine)):
            k = i - delay

            @pl.when((k >= 0) & (k < CHUNKS))
            def _(k=k, stage_of=stage_of):
                stage_of(k)

        return carry

    lax.fori_loop(0, CHUNKS + 4, step, 0)

    def finish(k, carry):
        for j in range(PIECES):
            e_copy(k, j).wait_send()
        self_copy(k).wait()
        return carry

    lax.fori_loop(0, CHUNKS, finish, 0)
    sent = asend.at[:, pl.ds(0, 90)]
    pltpu.make_async_copy(sent, sent, a_send).wait()
    got = out.at[:, pl.ds(0, 15 * CHUNKS * SLOTS), :]
    pltpu.make_async_copy(got, got, a_recv).wait()


def shards(coeffs, legendre, wavenumber, band_rows):
    hbm = pl.BlockSpec(memory_space=pltpu.HBM)
    anywhere = pl.BlockSpec(memory_space=pl.ANY)
    dma = pltpu.SemaphoreType.DMA
    sums = (CHUNKS, PIECES, FIELDS // PIECES, SLOTS, 128)
    return pl.pallas_call(
        kernel,
        out_shape=jax.ShapeDtypeStruct((6, 16 * CHUNKS * SLOTS, 128), jnp.bfloat16),
        in_specs=[hbm, hbm, hbm, hbm],
        out_specs=anywhere,
        scratch_shapes=[
            pltpu.SMEM(wavenumber.shape, jnp.int32),
            pltpu.SMEM(band_rows.shape, jnp.int32),
            pltpu.VMEM((44, 2, coeffs.shape[2]), jnp.bfloat16),
            pltpu.VMEM((CHUNKS, BLOCK, QUAD * FIELDS), jnp.bfloat16),
            pltpu.VMEM((16, CHUNKS, BLOCK, QUAD * FIELDS), jnp.bfloat16),
            pltpu.VMEM(legendre.shape, jnp.bfloat16),
            pltpu.VMEM((ROWS, QUAD * FIELDS), jnp.bfloat16),
            pltpu.VMEM((QUAD * FIELDS, ROWS), jnp.bfloat16),
            pltpu.VMEM((FIELDS * SLOTS, 128), jnp.float32),
            pltpu.VMEM(sums, jnp.bfloat16),
            pltpu.VMEM(sums, jnp.bfloat16),
            pltpu.VMEM((CHUNKS, FIELDS, SLOTS, 128), jnp.bfloat16),
            dma((CHUNKS,)),
            dma,
            dma((2,)),
            dma((7, CHUNKS)),
            dma((7, CHUNKS)),
            dma((8, CHUNKS)),
            dma((8, CHUNKS)),
            dma((CHUNKS, PIECES)),
            dma((CHUNKS, PIECES)),
            dma,
            dma,
            dma((CHUNKS,)),
        ],
        compiler_params=pltpu.CompilerParams(
            collective_id=0, has_side_effects=True, vmem_limit_bytes=48 * 1024 * 1024
        ),
        cost_estimate=pl.CostEstimate(
            flops=2 * 40 * ROWS * 96 * 256, bytes_accessed=20_000_000, transcendentals=0
        ),
    )(pltpu.with_memory_space_constraint(jnp.swapaxes(coeffs, 0, 1), pltpu.HBM), pltpu.with_memory_space_constraint(wavenumber, pltpu.HBM), band_rows, legendre)


def solution(mesh):
    in_specs = (P(None, "band", "mset"), P("mset", None, "band"), P("mset"), P("band"))
    out_specs = P("mset", None, "band")
    return jax.shard_map(shards, mesh=mesh, in_specs=in_specs, out_specs=out_specs, check_vma=False)
```

```python
import jax
import jax.numpy as jnp
from jax import lax
from jax.experimental import pallas as pl
from jax.experimental.pallas import tpu as pltpu
from jax.sharding import PartitionSpec as P

TRUNC = 1279
MESH = pl.DeviceIdType.MESH
CHUNKS = 5
GROUPS = 2
QUAD = 4
FIELDS = 96
ROWS = 704
MAIN = 40
BLOCK = 2 * MAIN + 8
SLOTS = 2 * GROUPS * QUAD
PIECES = 8
PEERS = 16 // PIECES
OFFSETS = (0, -1, 1, -2, 2, -3, 3, 4)


def kernel(
    coeffs, wavenumber, band_rows, legendre, out,
    wave_ref, rows_ref, raw, other, held, leg, natural, turned, stage, esend, erecv, asend,
    leg_sem, raw_sem, small_sem, z_send, z_recv, x_send, x_recv, e_send, e_recv, a_send, a_recv, self_sem,
):
    s = lax.axis_index("mset")
    b = lax.axis_index("band")
    xl, z = b // 8, b % 8
    parity = z % 2

    def at_z(offset):
        return lax.rem(z + (8 + offset), 8)

    def on_line(offset):
        return (s, xl * 8 + at_z(offset))

    def own_slot(offset):
        return xl * 8 + at_z(offset)

    across = (s, (1 - xl) * 8 + z)
    mirror = (s, xl * 8 + z + 1 - 2 * parity)

    barrier = pltpu.get_barrier_semaphore()
    for device in (on_line(-2), on_line(-1), on_line(1), on_line(2), across):
        pl.semaphore_signal(barrier, inc=1, device_id=device, device_id_type=MESH)

    def greet(d, carry):
        pl.semaphore_signal(barrier, inc=1, device_id=(lax.rem(s + d, 16), b), device_id_type=MESH)
        return carry

    lax.fori_loop(1, 16, greet, 0)

    def leg_copy(k):
        pairs = pl.ds(k * GROUPS * QUAD, GROUPS * QUAD)
        return pltpu.make_async_copy(legendre.at[pairs], leg.at[pairs], leg_sem.at[k])

    raw_copy = pltpu.make_async_copy(coeffs, raw, raw_sem)
    raw_copy.start()
    small_copies = [
        pltpu.make_async_copy(src, dst, small_sem.at[i])
        for i, (src, dst) in enumerate(((wavenumber, wave_ref), (band_rows, rows_ref)))
    ]
    for copy in small_copies:
        copy.start()
    for k in range(CHUNKS):
        leg_copy(k).start()
    raw_copy.wait()
    for copy in small_copies:
        copy.wait()

    def pack(k):
        both = []
        for i in range(GROUPS):
            start = pl.multiple_of((k * GROUPS + i) * (QUAD * FIELDS), QUAD * FIELDS)
            both.append(raw[:, :, pl.ds(start, QUAD * FIELDS)].astype(jnp.float32))

        def fill(put, p):
            parts = [values[:, p, :] for values in both]
            if parity_of == 0:
                mains, tails = [v[:MAIN] for v in parts], [v[MAIN:] for v in parts]
            else:
                mains, tails = [v[4:] for v in parts], [v[:4] for v in reversed(parts)]
            put(0, mains[0])
            put(MAIN, mains[1])
            put(2 * MAIN, jnp.concatenate(tails, 0))

        def put_own(row, values):
            held[own_slot(0), k, pl.ds(row, values.shape[0]), :] = values.astype(jnp.bfloat16)

        def put_other(row, values):
            other[k, pl.ds(row, values.shape[0]), :] = values.astype(jnp.bfloat16)

        for parity_of in range(2):

            @pl.when(parity == parity_of)
            def _():
                fill(put_own, parity_of)
                fill(put_other, 1 - parity_of)

    pack(0)
    pl.semaphore_wait(barrier, 20)

    def z_copy(kind, k):
        if kind == 4:
            way = 1 - 2 * lax.rem(k + s, 2)
            block, target = -2 * way, 2 * way
        else:
            block, target = {0: (0, 2), 1: (0, -2), 2: (0, 1), 3: (0, -1), 5: (-1, 2), 6: (1, -2)}[kind]
        src = other.at[k] if kind in (2, 3) else held.at[own_slot(block), k]
        return pltpu.make_async_remote_copy(
            src_ref=src,
            dst_ref=held.at[own_slot(block), k],
            send_sem=z_send.at[kind, k],
            recv_sem=z_recv.at[kind, k],
            device_id=on_line(target),
            device_id_type=MESH,
        )

    def z_arrival(kind, k):
        block = {0: -2, 1: 2, 2: -1, 3: 1, 4: 4, 5: -3, 6: 3}[kind]
        here = held.at[own_slot(block), k]
        return pltpu.make_async_copy(here, here, z_recv.at[kind, k])

    def x_copy(j, k):
        slot = own_slot(OFFSETS[j])
        return pltpu.make_async_remote_copy(
            src_ref=held.at[slot, k],
            dst_ref=held.at[slot, k],
            send_sem=x_send.at[j, k],
            recv_sem=x_recv.at[j, k],
            device_id=across,
            device_id_type=MESH,
        )

    def x_arrival(j, k):
        here = held.at[(1 - xl) * 8 + at_z(OFFSETS[j]), k]
        return pltpu.make_async_copy(here, here, x_recv.at[j, k])

    def e_copy(k, piece):
        return pltpu.make_async_remote_copy(
            src_ref=esend.at[k, piece],
            dst_ref=erecv.at[k, piece],
            send_sem=e_send.at[k, piece],
            recv_sem=e_recv.at[k, piece],
            device_id=mirror,
            device_id_type=MESH,
        )

    def out_rows(k):
        return pl.ds(pl.multiple_of(s * (CHUNKS * SLOTS) + k * SLOTS, SLOTS), SLOTS)

    def self_copy(k):
        return pltpu.make_async_copy(asend.at[k, pl.ds(s * 6, 6)], out.at[:, out_rows(k), :], self_sem.at[k])

    def direct(k):
        for kind in range(4):
            z_copy(kind, k).start()
        x_copy(0, k).start()

    def forward(k):
        for kind in (2, 3, 0, 1):
            z_arrival(kind, k).wait()
            if kind >= 2:
                z_copy(kind + 3, k).start()
            x_copy({2: 1, 3: 2, 0: 3, 1: 4}[kind], k).start()
        z_copy(4, k).start()

    def last(k):
        for kind, j in ((5, 5), (6, 6), (4, 7)):
            z_arrival(kind, k).wait()
            x_copy(j, k).start()

    def transform(k):
        for j in range(8):
            x_arrival(j, k).wait()
        leg_copy(k).wait()
        row = lax.broadcasted_iota(jnp.int32, (ROWS, 128), 0)
        upper = lax.broadcasted_iota(jnp.int32, (8, QUAD * FIELDS), 0) < 4
        for i in range(GROUPS):
            for j in range(8):
                start = j * 2 * 44
                for band, place in ((2 * j, start), (2 * j + 1, start + MAIN + 8)):
                    natural[pl.ds(place, MAIN), :] = held[band, k, pl.ds(i * MAIN, MAIN), :]
                tails = [held[band, k, pl.ds(2 * MAIN, 8), :].astype(jnp.float32) for band in (2 * j, 2 * j + 1)]
                if i == 0:
                    shared = jnp.where(upper, tails[0], tails[1])
                else:
                    shared = pltpu.roll(jnp.where(upper, tails[1], tails[0]), 4, 0)
                natural[pl.ds(start + MAIN, 8), :] = shared.astype(jnp.bfloat16)
            turned[...] = natural[...].T

            def pair(n, carry, i=i):
                q = (k * GROUPS + i) * QUAD + n
                m = wave_ref[q]
                first = jnp.maximum(lax.shift_right_arithmetic(TRUNC - m - parity, 1) + 1, 0)
                total = first + jnp.maximum(lax.shift_right_arithmetic(m - parity, 1) + 1, 0)
                values = leg[q]
                zero = jnp.zeros_like(values)
                low = jnp.where(row < first, values, zero)
                high = jnp.where((row >= first) & (row < total), values, zero)
                fields = turned[pl.ds(pl.multiple_of(n * FIELDS, FIELDS), FIELDS), :]
                sums = jnp.dot(
                    fields, jnp.concatenate([low, high], 1), preferred_element_type=jnp.float32
                )
                slot = i * (2 * QUAD) + 2 * n
                stage[pl.ds(slot, FIELDS, stride=SLOTS), :] = sums[:, :128]
                stage[pl.ds(slot + 1, FIELDS, stride=SLOTS), :] = sums[:, 128:]
                return carry

            lax.fori_loop(0, QUAD, pair, 0)
        esend[k] = stage[...].astype(jnp.bfloat16).reshape(esend.shape[1:])
        for j in range(PIECES):
            e_copy(k, piece_of(j)).start()

    def piece_of(j):
        return lax.rem(s // PEERS + 1 + j, PIECES)

    def combine(k):
        sign = jnp.where(parity == 0, 1.0, -1.0).astype(jnp.float32)
        lane = lax.broadcasted_iota(jnp.int32, esend.shape[2:], 2)

        def part(j, carry):
            piece = piece_of(j)
            e_copy(k, piece).wait_recv()
            grid = erecv[k, piece].astype(jnp.float32) + sign * esend[k, piece].astype(jnp.float32)
            columns = pl.ds(piece * (FIELDS // PIECES), FIELDS // PIECES)
            asend[k, columns] = jnp.where(lane < rows_ref[0], grid, 0.0).astype(jnp.bfloat16)

            def send(d, carry):
                t = piece * PEERS + lax.rem(s + 1 + d, PEERS)

                @pl.when(t != s)
                def _():
                    pltpu.make_async_remote_copy(
                        src_ref=asend.at[k, pl.ds(t * 6, 6)],
                        dst_ref=out.at[:, out_rows(k), :],
                        send_sem=a_send,
                        recv_sem=a_recv,
                        device_id=(t, b),
                        device_id_type=MESH,
                    ).start()

                @pl.when(t == s)
                def _():
                    self_copy(k).start()

                return carry

            return lax.fori_loop(0, PEERS, send, carry)

        lax.fori_loop(0, PIECES, part, 0)

    direct(0)

    def drain(k):
        for kind in range(7):
            z_copy(kind, k).wait_send()
        for j in range(8):
            x_copy(j, k).wait_send()

    def step(i, carry):
        @pl.when(i < CHUNKS)
        def _():
            forward(i)

        @pl.when(i + 1 < CHUNKS)
        def _():
            pack(i + 1)
            direct(i + 1)

        for delay, stage_of in ((1, last), (2, transform), (4, drain), (4, combine)):
            k = i - delay

            @pl.when((k >= 0) & (k < CHUNKS))
            def _(k=k, stage_of=stage_of):
                stage_of(k)

        return carry

    lax.fori_loop(0, CHUNKS + 4, step, 0)

    def finish(k, carry):
        for j in range(PIECES):
            e_copy(k, j).wait_send()
        self_copy(k).wait()
        return carry

    lax.fori_loop(0, CHUNKS, finish, 0)
    sent = asend.at[:, pl.ds(0, 90)]
    pltpu.make_async_copy(sent, sent, a_send).wait()
    got = out.at[:, pl.ds(0, 15 * CHUNKS * SLOTS), :]
    pltpu.make_async_copy(got, got, a_recv).wait()


def shards(coeffs, legendre, wavenumber, band_rows):
    hbm = pl.BlockSpec(memory_space=pltpu.HBM)
    anywhere = pl.BlockSpec(memory_space=pl.ANY)
    dma = pltpu.SemaphoreType.DMA
    sums = (CHUNKS, PIECES, FIELDS // PIECES, SLOTS, 128)
    return pl.pallas_call(
        kernel,
        out_shape=jax.ShapeDtypeStruct((6, 16 * CHUNKS * SLOTS, 128), jnp.bfloat16),
        in_specs=[hbm, hbm, hbm, hbm],
        out_specs=anywhere,
        scratch_shapes=[
            pltpu.SMEM(wavenumber.shape, jnp.int32),
            pltpu.SMEM(band_rows.shape, jnp.int32),
            pltpu.VMEM((44, 2, coeffs.shape[2]), jnp.bfloat16),
            pltpu.VMEM((CHUNKS, BLOCK, QUAD * FIELDS), jnp.bfloat16),
            pltpu.VMEM((16, CHUNKS, BLOCK, QUAD * FIELDS), jnp.bfloat16),
            pltpu.VMEM(legendre.shape, jnp.bfloat16),
            pltpu.VMEM((ROWS, QUAD * FIELDS), jnp.bfloat16),
            pltpu.VMEM((QUAD * FIELDS, ROWS), jnp.bfloat16),
            pltpu.VMEM((FIELDS * SLOTS, 128), jnp.float32),
            pltpu.VMEM(sums, jnp.bfloat16),
            pltpu.VMEM(sums, jnp.bfloat16),
            pltpu.VMEM((CHUNKS, FIELDS, SLOTS, 128), jnp.bfloat16),
            dma((CHUNKS,)),
            dma,
            dma((2,)),
            dma((7, CHUNKS)),
            dma((7, CHUNKS)),
            dma((8, CHUNKS)),
            dma((8, CHUNKS)),
            dma((CHUNKS, PIECES)),
            dma((CHUNKS, PIECES)),
            dma,
            dma,
            dma((CHUNKS,)),
        ],
        compiler_params=pltpu.CompilerParams(
            collective_id=0, has_side_effects=True, vmem_limit_bytes=48 * 1024 * 1024
        ),
        cost_estimate=pl.CostEstimate(
            flops=2 * 40 * ROWS * 96 * 256, bytes_accessed=20_000_000, transcendentals=0
        ),
    )(pltpu.with_memory_space_constraint(jnp.swapaxes(coeffs, 0, 1), pltpu.HBM), pltpu.with_memory_space_constraint(wavenumber, pltpu.HBM), band_rows, legendre)


def solution(mesh):
    in_specs = (P(None, "band", "mset"), P("mset", None, "band"), P("mset"), P("band"))
    out_specs = P("mset", None, "band")
    return jax.shard_map(shards, mesh=mesh, in_specs=in_specs, out_specs=out_specs, check_vma=False)
```
